32 devices in a mesh: rows: 8 (over z, y), rep: 4 (over x, core).
Axes of the slice: x: 2, y: 2, z: 4, core: 2. Of those that a mesh axis runs over, the one named last changes fastest.
Arguments:
- features: bfloat16 [32768, 512], P('rows', 'rep'), may hold values from -6 to 6
- adjacency: bfloat16 [256, 6, 128, 128], P('rows'), may hold values from -1 to 1
- neighbours: int32 [256, 6], P('rows'), may hold values from 0 to 47, as said below
- occupancy: int32 [256], P('rows'), may hold values from 32 to 128
- send_cells: int32 [8, 8, 2], P('rows'), may hold values from 0 to 31
- weight: bfloat16 [512, 512], replicated, may hold values from -0.25 to 0.25
- cotangent: bfloat16 [32768, 512], P('rows', 'rep'), may hold values from -6 to 6
Outputs:
- output: bfloat16 [32768, 512], P('rows', 'rep')
- weight_grad: float32 [512, 512], P('rep')
- feature_grad: bfloat16 [32768, 512], P('rows', 'rep')
The draws below stay inside these ranges and needn't reach their ends.
Inputs may be any that keep to these rules, and one draw needn't show every extreme that they name: neighbours[i,0] = i % 32, the cell itself; other entries name any slot.
All inputs are finite; a program needn't handle non-finite values.
Results may differ from the reference program's by a relative error of at most 0.0068.
Values may be sent and summed in bfloat16 or wider, within the bound.
A program may use at most 128 MiB of HBM per device.

```python
import jax
import jax.numpy as jnp
from jax import lax

F = 512
C = 128
NB = 6
SEND = 2
CELLS_DEV = 32
PEERS = 8
NCELL = 256
MOLECULES = 32768
SLOTS = 48
N_ROWS = 8


def draw_neighbours(key, part):
    key = jax.random.fold_in(key, 11)
    itself = (jnp.arange(NCELL, dtype=jnp.int32) % CELLS_DEV).astype(jnp.int32)
    others = jax.random.randint(key, (NCELL, NB - 1), 0, SLOTS, dtype=jnp.int32)
    others = others.at[0, 0].set(SLOTS - 1)
    return jnp.concatenate([itself[:, None], others], axis=1)


def draw_occupancy(key, part):
    key = jax.random.fold_in(key, 23)
    counts = jax.random.randint(key, (NCELL,), C // 4, C + 1, dtype=jnp.int32)
    counts = counts.at[0].set(C)
    counts = counts.at[1].set(C // 4)
    return counts


def with_ends(entries, rng, low, top_value):
    longest = entries.shape.index(max(entries.shape))
    spots = []
    for shift in (0, 1):
        where = [jax.random.randint(jax.random.fold_in(rng, axis), (), 0, length) for axis, length in enumerate(entries.shape)]
        where[longest] = (where[longest] + shift) % entries.shape[longest]
        spots.append(tuple(where))
    return entries.at[spots[0]].set(low).at[spots[1]].set(top_value)


def block_levels(stream_key, dims, cuts, least, largest):
    loudness = 1.0
    for axis_at, blocks in cuts:
        draws = jax.random.uniform(jax.random.fold_in(jax.random.fold_in(stream_key, 6), axis_at), (blocks,), jnp.float32, least / len(cuts), largest / len(cuts))
        loudness = loudness * jnp.repeat(jnp.exp(draws), dims[axis_at] // blocks).reshape((-1,) + (1,) * (len(dims) - 1 - axis_at))
    return loudness


def bell_draw(key, dims, deviation, limit, split=(), kind=jnp.bfloat16):
    entries = deviation * jax.random.normal(key, dims, jnp.float32)
    if split:
        entries = entries * block_levels(key, dims, split, -0.22, 0.18)
    return jnp.clip(entries, -limit, limit).astype(kind)


def setup_inputs(seed: int = 0) -> dict:
    keys = jax.random.split(jax.random.key(seed), 8)
    return {
        "features": bell_draw(keys[0], (MOLECULES, F), 1.0, 6.0, ((0, 8), (1, 4))),
        "adjacency": jnp.clip(jax.random.uniform(keys[1], (NCELL, NB, C, C), jnp.float32, -1.0, 1.0) * block_levels(keys[1], (NCELL, NB, C, C), ((0, 8),), -0.4, 0.0), -1.0, 1.0).astype(jnp.bfloat16),
        "neighbours": draw_neighbours(jax.random.fold_in(keys[7], 71), 0),
        "occupancy": draw_occupancy(jax.random.fold_in(keys[7], 71), 0),
        "send_cells": with_ends(jax.random.randint(keys[4], (PEERS, PEERS, SEND), 0, CELLS_DEV), jax.random.fold_in(keys[4], 1), 0, CELLS_DEV - 1).astype(jnp.int32),
        "weight": bell_draw(keys[5], (F, F), F ** -0.5, 0.25),
        "cotangent": bell_draw(keys[6], (MOLECULES, F), 1.0, 6.0, ((0, 8), (1, 4))),
    }


def reference(features, adjacency, neighbours, occupancy, send_cells, weight, cotangent):
    ncell = adjacency.shape[0]
    slot_ids = jnp.arange(C, dtype=jnp.int32)
    mask = (slot_ids[None, :] < occupancy[:, None]).astype(jnp.float32)
    cell_ids = jnp.arange(ncell, dtype=jnp.int32)
    owner = (cell_ids // CELLS_DEV).astype(jnp.int32)
    offset = jnp.maximum(neighbours - CELLS_DEV, 0).astype(jnp.int32)
    sender = (offset // SEND).astype(jnp.int32)
    within = (offset % SEND).astype(jnp.int32)
    remote = sender * CELLS_DEV + send_cells[sender, owner[:, None] * jnp.ones_like(sender), within]
    source = jnp.where(neighbours < CELLS_DEV, owner[:, None] * CELLS_DEV + neighbours, remote).astype(jnp.int32)
    adj_dev = adjacency.reshape(N_ROWS, CELLS_DEV, NB, C, C)

    def row_scale(block):
        values = block.astype(jnp.float32)
        return (jnp.sum(values * values, axis=(1, 3)) + 1e-6) ** -0.25

    scale = lax.map(row_scale, adj_dev).reshape(ncell, C)
    keep = scale * mask
    scaled = (features.reshape(ncell, C, F).astype(jnp.float32) * keep[..., None]).astype(jnp.bfloat16)

    def aggregate(args):
        block, ids, sc = args
        near = scaled[ids].astype(jnp.float32)
        total = jnp.einsum('ikrc,ikcf->irf', block.astype(jnp.float32), near)
        return (total * sc[..., None]).astype(jnp.bfloat16)

    aggregated = lax.map(aggregate, (adj_dev, source.reshape(N_ROWS, CELLS_DEV, NB), scale.reshape(N_ROWS, CELLS_DEV, C)))
    aggregated = aggregated.reshape(ncell * C, F)
    mask_rows = mask.reshape(-1)[:, None]
    pre = jnp.dot(aggregated, weight, preferred_element_type=jnp.float32)
    output = (mask_rows * jax.nn.silu(pre)).astype(jnp.bfloat16)
    sig = jax.nn.sigmoid(pre)
    slope = (cotangent.astype(jnp.float32) * mask_rows * sig * (1.0 + pre * (1.0 - sig))).astype(jnp.bfloat16)
    weight_grad = jnp.dot(aggregated.T, slope, preferred_element_type=jnp.float32) * (float(ncell * C) ** -0.5)
    back = jnp.dot(slope, weight.T, preferred_element_type=jnp.float32)
    upstream = (back * scale.reshape(-1)[:, None]).astype(jnp.bfloat16).reshape(N_ROWS, CELLS_DEV, C, F)
    slot_range = jnp.arange(N_ROWS * SEND, dtype=jnp.int32)
    slot_peer = (slot_range // SEND).astype(jnp.int32)
    slot_within = (slot_range % SEND).astype(jnp.int32)
    local_ids = jnp.arange(CELLS_DEV, dtype=jnp.int32)

    def spread(total, args):
        block, ids, term, device = args
        contrib = jnp.einsum('ikrc,irf->ikcf', block.astype(jnp.float32), term.astype(jnp.float32))
        slot_sum = jax.ops.segment_sum(contrib.reshape(-1, C, F), ids.reshape(-1), num_segments=CELLS_DEV + N_ROWS * SEND)
        local_part = slot_sum[:CELLS_DEV]
        rounded = lax.optimization_barrier(slot_sum[CELLS_DEV:].astype(jnp.bfloat16))
        owners = (slot_peer * CELLS_DEV + send_cells[slot_peer, device * jnp.ones_like(slot_peer), slot_within]).astype(jnp.int32)
        total = total.at[(device * CELLS_DEV + local_ids).astype(jnp.int32)].add(local_part)
        total = total.at[owners].add(rounded.astype(jnp.float32))
        return total, None

    devices = jnp.arange(N_ROWS, dtype=jnp.int32)
    gathered, _ = lax.scan(spread, jnp.zeros((ncell, C, F), jnp.float32), (adj_dev, neighbours.reshape(N_ROWS, CELLS_DEV, NB), upstream, devices))
    feature_grad = (gathered * keep[..., None]).astype(jnp.bfloat16).reshape(ncell * C, F)
    return output, weight_grad, feature_grad
```

```python
import functools

import jax
import jax.numpy as jnp
from jax import lax
from jax.experimental import pallas as pl
from jax.experimental.pallas import tpu as pltpu
from jax.sharding import PartitionSpec as P

MESH = pl.DeviceIdType.MESH
F32 = jnp.float32
BF16 = jnp.bfloat16
SMEM = pltpu.SMEM
VMEM = pltpu.VMEM


def params(**kw):
    return pltpu.CompilerParams(vmem_limit_bytes=56 * 1024 * 1024, **kw)


def whole_block(shape):
    return pl.BlockSpec(shape, lambda *_: (0,) * len(shape))


def row_mask(count, slots):
    rows = lax.broadcasted_iota(jnp.int32, (slots, 1), 0)
    return jnp.where(rows < count, 1.0, 0.0).astype(F32)


def prepare_body(step_cells, occ, send, feat, adj, scale_out, scaled_out, outgoing):
    step = pl.program_id(0)
    slots = adj.shape[2]
    for j in range(step_cells):
        cell = step * step_cells + j
        total = jnp.zeros((slots, slots), F32)
        for k in range(adj.shape[1]):
            a = adj[j, k].astype(F32)
            total += a * a
        s = jnp.sum(total, axis=1, keepdims=True) + 1e-6
        scale = lax.rsqrt(jnp.sqrt(s))
        scale_out[j] = jnp.broadcast_to(scale, scale_out.shape[1:])
        keep = scale * row_mask(occ[cell], slots)
        scaled_out[cell] = (feat[j].astype(F32) * keep).astype(BF16)

    @pl.when(step == pl.num_programs(0) - 1)
    def _():
        def put(t, carry):
            outgoing[t] = scaled_out[send[t]]
            return carry

        lax.fori_loop(0, outgoing.shape[0], put, 0)


def prepare(features, adjacency, occupancy, send):
    cells, blocks, slots, _ = adjacency.shape
    part = features.shape[2]
    n = 4
    count = send.shape[0]
    return pl.pallas_call(
        functools.partial(prepare_body, n),
        grid=(cells // n,),
        in_specs=[
            pl.BlockSpec(memory_space=SMEM),
            pl.BlockSpec(memory_space=SMEM),
            pl.BlockSpec((n, slots, part), lambda i: (i, 0, 0)),
            pl.BlockSpec((n, blocks, slots, slots), lambda i: (i, 0, 0, 0)),
        ],
        out_specs=[
            pl.BlockSpec((n, slots, part), lambda i: (i, 0, 0)),
            whole_block((cells, slots, part)),
            whole_block((count, slots, part)),
        ],
        out_shape=[
            jax.ShapeDtypeStruct((cells, slots, part), F32),
            jax.ShapeDtypeStruct((cells, slots, part), BF16),
            jax.ShapeDtypeStruct((count, slots, part), BF16),
        ],
        compiler_params=params(),
        name="prepare",
    )(occupancy, send, features, adjacency)


def aggregate_body(step_cells, neigh, scaled, incoming, scale, adj, out, table):
    step = pl.program_id(0)
    blocks = adj.shape[1]
    cells = scaled.shape[0]

    @pl.when(step == 0)
    def _():
        table[pl.ds(0, cells)] = scaled[...]
        table[pl.ds(cells, incoming.shape[0])] = incoming[...]

    for j in range(step_cells):
        cell = step * step_cells + j
        near = jnp.concatenate([table[neigh[cell * blocks + k]] for k in range(blocks)], axis=0)
        wide = jnp.concatenate([adj[j, k] for k in range(blocks)], axis=1)
        total = jnp.dot(wide, near, preferred_element_type=F32)
        out[j] = (total * scale[j]).astype(BF16)


def aggregate(neigh, scaled, incoming, scale, adjacency):
    cells, blocks, slots, _ = adjacency.shape
    part = scaled.shape[2]
    n = 4
    return pl.pallas_call(
        functools.partial(aggregate_body, n),
        grid=(cells // n,),
        in_specs=[
            pl.BlockSpec(memory_space=SMEM),
            whole_block(scaled.shape),
            whole_block(incoming.shape),
            pl.BlockSpec((n, slots, part), lambda i: (i, 0, 0)),
            pl.BlockSpec((n, blocks, slots, slots), lambda i: (i, 0, 0, 0)),
        ],
        out_specs=pl.BlockSpec((n, slots, part), lambda i: (i, 0, 0)),
        out_shape=jax.ShapeDtypeStruct((cells, slots, part), BF16),
        scratch_shapes=[VMEM((cells + incoming.shape[0], slots, part), BF16)],
        compiler_params=params(),
        name="aggregate",
    )(neigh, scaled, incoming, scale, adjacency)


def middle_body(step_cells, first, occ, agg, cot, scale, weight, out, up, wgrad, acc):
    step = pl.program_id(0)
    reps, rows, part = agg.shape
    slots = rows // step_cells
    base = first[0] + step * step_cells
    a = jnp.concatenate([agg[q] for q in range(reps)], axis=1)
    pre = jnp.dot(a, weight[...], preferred_element_type=F32)
    mask = jnp.concatenate([row_mask(occ[base + j], slots) for j in range(step_cells)], axis=0)
    sig = 0.5 * jnp.tanh(0.5 * pre) + 0.5
    o = (mask * (pre * sig)).astype(BF16)
    c = jnp.concatenate([cot[q] for q in range(reps)], axis=1).astype(F32)
    slope = (c * mask * sig * (1.0 + pre * (1.0 - sig))).astype(BF16)
    back = lax.dot_general(slope, weight[...], (((1,), (1,)), ((), ())), preferred_element_type=F32)
    s = scale[...].reshape(rows, part)
    for q in range(reps):
        cols = slice(q * part, (q + 1) * part)
        out[q] = o[:, cols]
        up[q] = (back[:, cols] * s).astype(BF16)
    term = lax.dot_general(a, slope, (((0,), (0,)), ((), ())), preferred_element_type=F32)

    @pl.when(step == 0)
    def _():
        acc[...] = term

    @pl.when(step > 0)
    def _():
        acc[...] += term

    @pl.when(step == pl.num_programs(0) - 1)
    def _():
        wgrad[...] = acc[...].astype(BF16)


def middle(first, occupancy, agg, cot, scale, weight):
    reps, rows, part = agg.shape
    slots = scale.shape[1]
    n = 2
    step_rows = n * slots
    width = weight.shape[1]
    row_block = pl.BlockSpec((reps, step_rows, part), lambda i, f: (0, i, 0))
    return pl.pallas_call(
        functools.partial(middle_body, n),
        grid_spec=pltpu.PrefetchScalarGridSpec(
            num_scalar_prefetch=1,
            grid=(rows // step_rows,),
            in_specs=[
                pl.BlockSpec(memory_space=SMEM),
                row_block,
                row_block,
                pl.BlockSpec((n, slots, part), lambda i, f: (f[0] // n + i, 0, 0)),
                whole_block(weight.shape),
            ],
            out_specs=[row_block, row_block, whole_block(weight.shape)],
            scratch_shapes=[VMEM((reps * part, width), F32)],
        ),
        out_shape=[
            jax.ShapeDtypeStruct((reps, rows, part), BF16),
            jax.ShapeDtypeStruct((reps, rows, part), BF16),
            jax.ShapeDtypeStruct(weight.shape, BF16),
        ],
        compiler_params=params(),
        name="middle",
    )(first, occupancy, agg, cot, scale, weight)


def spread_body(step_cells, neigh, up, adj, local, remote, table):
    step = pl.program_id(0)
    blocks, slots = adj.shape[1], adj.shape[2]

    @pl.when(step == 0)
    def _():
        table[...] = jnp.zeros_like(table)

    for j in range(step_cells):
        cell = step * step_cells + j
        wide = jnp.concatenate([adj[j, k] for k in range(blocks)], axis=1)
        terms = lax.dot_general(wide, up[j], (((0,), (0,)), ((), ())), preferred_element_type=F32)
        for k in range(blocks):
            slot = neigh[cell * blocks + k]
            table[slot] = table[slot] + terms[k * slots : (k + 1) * slots]

    @pl.when(step == pl.num_programs(0) - 1)
    def _():
        cells = local.shape[0]
        local[...] = table[pl.ds(0, cells)]
        remote[...] = table[pl.ds(cells, remote.shape[0])].astype(BF16)


def spread(neigh, up, adjacency, received):
    cells, blocks, slots, _ = adjacency.shape
    part = up.shape[2]
    n = 4
    return pl.pallas_call(
        functools.partial(spread_body, n),
        grid=(cells // n,),
        in_specs=[
            pl.BlockSpec(memory_space=SMEM),
            pl.BlockSpec((n, slots, part), lambda i: (i, 0, 0)),
            pl.BlockSpec((n, blocks, slots, slots), lambda i: (i, 0, 0, 0)),
        ],
        out_specs=[whole_block((cells, slots, part)), whole_block((received, slots, part))],
        out_shape=[
            jax.ShapeDtypeStruct((cells, slots, part), F32),
            jax.ShapeDtypeStruct((received, slots, part), BF16),
        ],
        scratch_shapes=[VMEM((cells + received, slots, part), F32)],
        compiler_params=params(),
        name="spread",
    )(neigh, up, adjacency)


def combine_body(send, occ, local, returned, scale, out, total):
    slots = local.shape[1]
    total[...] = local[...]

    def add(t, carry):
        cell = send[t]
        total[cell] = total[cell] + returned[t].astype(F32)
        return carry

    lax.fori_loop(0, returned.shape[0], add, 0)

    def finish(i, carry):
        out[i] = (total[i] * (scale[i] * row_mask(occ[i], slots))).astype(BF16)
        return carry

    lax.fori_loop(0, local.shape[0], finish, 0)


def combine(send, occupancy, local, returned, scale):
    return pl.pallas_call(
        combine_body,
        in_specs=[pl.BlockSpec(memory_space=SMEM)] * 2 + [pl.BlockSpec(memory_space=VMEM)] * 3,
        out_specs=pl.BlockSpec(memory_space=VMEM),
        out_shape=jax.ShapeDtypeStruct(local.shape, BF16),
        scratch_shapes=[VMEM(local.shape, F32)],
        compiler_params=params(),
        name="combine",
    )(send, occupancy, local, returned, scale)


def greet(axes):
    barrier = pltpu.get_barrier_semaphore()
    expected = 0
    for axis in axes:
        size = lax.axis_size(axis)
        me = lax.axis_index(axis)
        for d in range(1, size):
            pl.semaphore_signal(
                barrier, inc=1, device_id={axis: lax.rem(me + d, size)}, device_id_type=MESH
            )
        expected += size - 1
    pl.semaphore_wait(barrier, expected)


def start_exchange(axis, src, dst, sends, recvs, own):
    size = lax.axis_size(axis)
    me = lax.axis_index(axis)
    copies = []
    for d in range(1, size):
        peer = lax.rem(me + d, size)
        copy = pltpu.make_async_remote_copy(
            src_ref=src.at[peer],
            dst_ref=dst.at[me],
            send_sem=sends.at[d],
            recv_sem=recvs.at[d],
            device_id={axis: peer},
            device_id_type=MESH,
        )
        copy.start()
        copies.append(copy)
    mine = pltpu.make_async_copy(src.at[me], dst.at[me], own)
    mine.start()
    copies.append(mine)
    return copies


def exchange_body(axes, *refs):
    n = len(axes)
    srcs, dsts, sems = refs[:n], refs[n : 2 * n], refs[2 * n :]
    greet(sorted(set(axes)))
    copies = []
    for i, axis in enumerate(axes):
        copies += start_exchange(axis, srcs[i], dsts[i], sems[3 * i], sems[3 * i + 1], sems[3 * i + 2])
    for copy in copies:
        copy.wait()


def exchange_sems(axes):
    sems = []
    for axis in axes:
        size = lax.axis_size(axis)
        sems += [
            pltpu.SemaphoreType.DMA((size,)),
            pltpu.SemaphoreType.DMA((size,)),
            pltpu.SemaphoreType.DMA,
        ]
    return sems


def exchange(axes, arrays, collective_id, name):
    return pl.pallas_call(
        functools.partial(exchange_body, axes),
        in_specs=[pl.BlockSpec(memory_space=pl.ANY)] * len(arrays),
        out_specs=[pl.BlockSpec(memory_space=pl.ANY)] * len(arrays),
        out_shape=[jax.ShapeDtypeStruct(a.shape, a.dtype) for a in arrays],
        scratch_shapes=exchange_sems(axes),
        compiler_params=params(collective_id=collective_id, has_side_effects=True),
        name=name,
    )(*arrays)


def last_body(factor, terms, out_rows, wgrad, returned, out, grad, ph1, held, ph2, *sems):
    greet(("rep", "rows"))
    first = start_exchange("rep", wgrad, ph1, *sems[0:3])
    others = start_exchange("rows", terms, returned, *sems[3:6])
    others += start_exchange("rep", out_rows, out, *sems[6:9])
    for copy in first:
        copy.wait()
    total = ph1[0].astype(F32)
    for q in range(1, ph1.shape[0]):
        total += ph1[q].astype(F32)
    peers = lax.axis_size("rows")
    if ph2 is None:
        grad[...] = total
    else:
        held[...] = total.astype(BF16).reshape(held.shape)
        for copy in start_exchange("rows", held, ph2, *sems[9:12]):
            copy.wait()
        total = ph2[0].astype(F32)
        for p in range(1, peers):
            total += ph2[p].astype(F32)
        me = lax.axis_index("rows")
        grad[me] = total * factor
        copies = []
        for d in range(1, peers):
            copy = pltpu.make_async_remote_copy(
                src_ref=grad.at[me],
                dst_ref=grad.at[me],
                send_sem=sems[12].at[d],
                recv_sem=sems[13].at[d],
                device_id={"rows": lax.rem(me + d, peers)},
                device_id_type=MESH,
            )
            copy.start()
            copies.append(copy)
        for copy in copies:
            copy.wait()
    for copy in others:
        copy.wait()


def last_exchange(terms, out_rows, wgrad, factor, collective_id):
    peers = lax.axis_size("rows")
    reps, part, width = wgrad.shape
    cut = part % (16 * peers) == 0
    axes = ("rep", "rows", "rep", "rows")
    scratch = [VMEM(wgrad.shape, BF16)]
    if cut:
        scratch += [VMEM((peers, part // peers, width), BF16)] * 2
        grad_shape = (peers, part // peers, width)
        scratch += exchange_sems(axes)
        scratch += [pltpu.SemaphoreType.DMA((peers,))] * 2
        body = functools.partial(last_body, factor)
    else:
        grad_shape = (part, width)
        scratch += exchange_sems(axes[:3])

        def body(t, o, w, r, out, grad, ph1, *sems):
            last_body(factor, t, o, w, r, out, grad, ph1, None, None, *sems)

    returned, out, grad = pl.pallas_call(
        body,
        in_specs=[pl.BlockSpec(memory_space=pl.ANY)] * 3,
        out_specs=[pl.BlockSpec(memory_space=pl.ANY)] * 2 + [pl.BlockSpec(memory_space=VMEM)],
        out_shape=[
            jax.ShapeDtypeStruct(terms.shape, BF16),
            jax.ShapeDtypeStruct(out_rows.shape, BF16),
            jax.ShapeDtypeStruct(grad_shape, F32),
        ],
        scratch_shapes=scratch,
        compiler_params=params(collective_id=collective_id, has_side_effects=True),
        name="last_exchange",
    )(terms, out_rows, wgrad)
    if not cut:
        grad = lax.psum(grad, "rows") * factor
    return returned, out, grad.reshape(part, width)


def on_device(features, adjacency, neighbours, occupancy, send_cells, weight, cotangent):
    cells, blocks, slots, _ = adjacency.shape
    part = features.shape[1]
    peers, reps = lax.axis_size("rows"), lax.axis_size("rep")
    sending = send_cells.shape[2]
    rows = cells * slots
    share = rows // reps
    send = send_cells.reshape(-1)
    neigh = neighbours.reshape(-1)
    table = (peers, sending * slots, part)
    cell_shape = (cells, slots, part)

    scale, scaled, outgoing = prepare(features.reshape(cell_shape), adjacency, occupancy, send)
    incoming, cot = exchange(
        ("rows", "rep"),
        (outgoing.reshape(table), cotangent.reshape(reps, share, part)),
        1,
        "first_exchange",
    )
    agg = aggregate(neigh, scaled, incoming.reshape(-1, slots, part), scale, adjacency)
    (agg_rows,) = exchange(("rep",), (agg.reshape(reps, share, part),), 2, "to_rows")
    first = (lax.axis_index("rep") * (cells // reps)).astype(jnp.int32).reshape(1)
    out_rows, up_rows, wgrad = middle(first, occupancy, agg_rows, cot, scale, weight)
    (up,) = exchange(("rep",), (up_rows,), 3, "to_columns")
    local, remote = spread(neigh, up.reshape(cell_shape), adjacency, peers * sending)
    factor = float(rows * peers) ** (-0.5)
    returned, output, weight_grad = last_exchange(
        remote.reshape(table), out_rows, wgrad.reshape(reps, part, -1), factor, 4
    )
    feature_grad = combine(send, occupancy, local, returned.reshape(-1, slots, part), scale)
    return output.reshape(rows, part), weight_grad, feature_grad.reshape(rows, part)


def solution(mesh):
    placed = (
        P("rows", "rep"),
        P("rows", None, None, None),
        P("rows", None),
        P("rows"),
        P("rows", None, None),
        P(),
        P("rows", "rep"),
    )
    return jax.shard_map(
        on_device,
        mesh=mesh,
        in_specs=placed,
        out_specs=(P("rows", "rep"), P("rep", None), P("rows", "rep")),
        check_vma=False,
    )
```

```python
import functools

import jax
import jax.numpy as jnp
from jax import lax
from jax.experimental import pallas as pl
from jax.experimental.pallas import tpu as pltpu
from jax.sharding import PartitionSpec as P

MESH = pl.DeviceIdType.MESH
F32 = jnp.float32
BF16 = jnp.bfloat16
SMEM = pltpu.SMEM
VMEM = pltpu.VMEM


def params(**kw):
    return pltpu.CompilerParams(vmem_limit_bytes=56 * 1024 * 1024, **kw)


def whole_block(shape):
    return pl.BlockSpec(shape, lambda *_: (0,) * len(shape))


def row_mask(count, slots):
    rows = lax.broadcasted_iota(jnp.int32, (slots, 1), 0)
    return jnp.where(rows < count, 1.0, 0.0).astype(F32)


def spread_body(step_cells, neigh, up, adj, local, remote, table):
    step = pl.program_id(0)
    blocks, slots = adj.shape[1], adj.shape[2]

    @pl.when(step == 0)
    def _():
        table[...] = jnp.zeros_like(table)

    for j in range(step_cells):
        cell = step * step_cells + j
        wide = jnp.concatenate([adj[j, k] for k in range(blocks)], axis=1)
        terms = lax.dot_general(wide, up[j], (((0,), (0,)), ((), ())), preferred_element_type=F32)
        for k in range(blocks):
            slot = neigh[cell, k]
            table[slot] = table[slot] + terms[k * slots : (k + 1) * slots]

    @pl.when(step == pl.num_programs(0) - 1)
    def _():
        cells = local.shape[0]
        local[...] = table[pl.ds(0, cells)]
        remote[...] = table[pl.ds(cells, remote.shape[0])].astype(BF16)


def spread(neigh, up, adjacency, received):
    cells, blocks, slots, _ = adjacency.shape
    part = up.shape[2]
    n = 4
    return pl.pallas_call(
        functools.partial(spread_body, n),
        grid=(cells // n,),
        in_specs=[
            pl.BlockSpec(memory_space=SMEM),
            pl.BlockSpec((n, slots, part), lambda i: (i, 0, 0)),
            pl.BlockSpec((n, blocks, slots, slots), lambda i: (i, 0, 0, 0)),
        ],
        out_specs=[whole_block((cells, slots, part)), whole_block((received, slots, part))],
        out_shape=[
            jax.ShapeDtypeStruct((cells, slots, part), F32),
            jax.ShapeDtypeStruct((received, slots, part), BF16),
        ],
        scratch_shapes=[VMEM((cells + received, slots, part), F32)],
        compiler_params=params(),
        cost_estimate=pl.CostEstimate(
            flops=2 * adjacency.size * part,
            bytes_accessed=30_000_000,
            transcendentals=0,
        ),
        name="spread",
    )(neigh, up, adjacency)


def greet(axes):
    barrier = pltpu.get_barrier_semaphore()
    expected = 0
    for axis in axes:
        size = lax.axis_size(axis)
        me = lax.axis_index(axis)
        for d in range(1, size):
            pl.semaphore_signal(
                barrier, inc=1, device_id={axis: lax.rem(me + d, size)}, device_id_type=MESH
            )
        expected += size - 1
    pl.semaphore_wait(barrier, expected)


def exchange_copies(axis, src, dst, sends, recvs):
    size = lax.axis_size(axis)
    me = lax.axis_index(axis)
    copies = []
    for d in range(1, size):
        peer = lax.rem(me + d, size)
        copies.append(
            pltpu.make_async_remote_copy(
                src_ref=src.at[peer],
                dst_ref=dst.at[me],
                send_sem=sends.at[d],
                recv_sem=recvs.at[d],
                device_id={axis: peer},
                device_id_type=MESH,
            )
        )
    copies.append(pltpu.make_async_copy(src.at[me], dst.at[me], recvs.at[0]))
    return copies


def start_all(copies):
    for copy in copies:
        copy.start()
    return copies


def wait_all(copies):
    for copy in copies:
        copy.wait()


def dma(*shape):
    return pltpu.SemaphoreType.DMA(shape)


def prepare_body(
    step_cells, occ, send, feat, adj, cot, scale_out, scaled_out, incoming, cot_in, outgoing, *sems
):
    step = pl.program_id(0)
    slots = adj.shape[2]
    sending = outgoing.shape[1]

    @pl.when(step == 0)
    def _():
        greet(("rep", "rows"))
        start_all(exchange_copies("rep", cot, cot_in, sems[0], sems[1]))

    for j in range(step_cells):
        cell = step * step_cells + j
        total = jnp.zeros((slots, slots), F32)
        for k in range(adj.shape[1]):
            a = adj[j, k].astype(F32)
            total += a * a
        scale = lax.rsqrt(jnp.sqrt(jnp.sum(total, axis=1, keepdims=True) + 1e-6))
        scale_out[j] = jnp.broadcast_to(scale, scale_out.shape[1:])
        keep = scale * row_mask(occ[cell], slots)
        scaled_out[cell] = (feat[j].astype(F32) * keep).astype(BF16)

    @pl.when(step == pl.num_programs(0) - 1)
    def _():
        def put(t, carry):
            peer, place = t // sending, t % sending
            outgoing[peer, place] = scaled_out[send[0, peer, place]]
            return carry

        lax.fori_loop(0, outgoing.shape[0] * sending, put, 0)
        copies = start_all(exchange_copies("rows", outgoing, incoming, sems[2], sems[3]))
        wait_all(copies)
        wait_all(exchange_copies("rep", cot, cot_in, sems[0], sems[1]))


def prepare(features, adjacency, occupancy, send, cot, collective_id):
    cells, blocks, slots, _ = adjacency.shape
    part = features.shape[2]
    n = 4
    _, peers, sending = send.shape
    table = (peers, sending, slots, part)
    reps = cot.shape[0]
    return pl.pallas_call(
        functools.partial(prepare_body, n),
        grid=(cells // n,),
        in_specs=[
            pl.BlockSpec(memory_space=SMEM),
            pl.BlockSpec(memory_space=SMEM),
            pl.BlockSpec((n, slots, part), lambda i: (i, 0, 0)),
            pl.BlockSpec((n, blocks, slots, slots), lambda i: (i, 0, 0, 0)),
            pl.BlockSpec(memory_space=pl.ANY),
        ],
        out_specs=[
            pl.BlockSpec((n, slots, part), lambda i: (i, 0, 0)),
            whole_block((cells, slots, part)),
            pl.BlockSpec(memory_space=pl.ANY),
            pl.BlockSpec(memory_space=pl.ANY),
        ],
        out_shape=[
            jax.ShapeDtypeStruct((cells, slots, part), F32),
            jax.ShapeDtypeStruct((cells, slots, part), BF16),
            jax.ShapeDtypeStruct(table, BF16),
            jax.ShapeDtypeStruct(cot.shape, BF16),
        ],
        scratch_shapes=[VMEM(table, BF16), dma(reps), dma(reps), dma(peers), dma(peers)],
        compiler_params=params(collective_id=collective_id, has_side_effects=True),
        name="prepare",
    )(occupancy, send, features, adjacency, cot)


def core_body(groups, neigh, occ, scaled_h, incoming_h, scale_h, adj_h, cot_h, weight_h, *refs):
    reps, rows, part = cot_h.shape
    up, outs, wgrads = refs[0], refs[1 : 1 + reps], refs[1 + reps : 1 + 2 * reps]
    table, scale, adj, cot, weight, agg, agg_in, slope_all, back_all, out_all, wgrad = refs[
        1 + 2 * reps : 12 + 2 * reps
    ]
    loads, adj_loads, send1, recv1, send2, recv2, stores = refs[12 + 2 * reps :]
    me = lax.axis_index("rep")
    cells, blocks, slots, _ = adj.shape
    per_rep = cells // reps
    per_group = per_rep // groups
    size = per_group * slots
    order = list(range(1, reps)) + [0]

    early = [
        pltpu.make_async_copy(scaled_h, table.at[pl.ds(0, cells)], loads.at[0]),
        pltpu.make_async_copy(
            incoming_h, table.at[pl.ds(cells, incoming_h.shape[0])], loads.at[1]
        ),
        pltpu.make_async_copy(scale_h, scale, loads.at[2]),
    ]
    start_all(early)
    adj_copies = {}
    for g in range(groups):
        for d in order:
            cell = lax.rem(me + d, reps) * per_rep + g * per_group
            span = pl.ds(cell, per_group)
            copy = pltpu.make_async_copy(adj_h.at[span], adj.at[span], adj_loads.at[g, d])
            copy.start()
            adj_copies[g, d] = copy
    late = start_all(
        [
            pltpu.make_async_copy(cot_h, cot, loads.at[3]),
            pltpu.make_async_copy(weight_h, weight, loads.at[4]),
        ]
    )
    greet(("rep",))
    wait_all(early)

    def copies_of(g, src, dst, sends, recvs):
        span = pl.ds(g * size, size)
        found = []
        for d in order:
            peer = lax.rem(me + d, reps)
            if d == 0:
                found.append(
                    pltpu.make_async_copy(src.at[me, span], dst.at[me, span], recvs.at[g, 0])
                )
                continue
            found.append(
                pltpu.make_async_remote_copy(
                    src_ref=src.at[peer, span],
                    dst_ref=dst.at[me, span],
                    send_sem=sends.at[g, d],
                    recv_sem=recvs.at[g, d],
                    device_id={"rep": peer},
                    device_id_type=MESH,
                )
            )
        return found

    forward = []
    for g in range(groups):
        copies = copies_of(g, agg, agg_in, send1, recv1)
        for i, d in enumerate(order):
            peer = lax.rem(me + d, reps)
            adj_copies[g, d].wait()
            for j in range(per_group):
                cell = peer * per_rep + g * per_group + j
                near = jnp.concatenate([table[neigh[cell, k]] for k in range(blocks)], axis=0)
                wide = jnp.concatenate([adj[cell, k] for k in range(blocks)], axis=1)
                total = jnp.dot(wide, near, preferred_element_type=F32)
                agg[peer, pl.ds(g * size + j * slots, slots)] = (total * scale[cell]).astype(BF16)
            copies[i].start()
        forward.append(copies)
    wait_all(late)
    backward = []
    for g in range(groups):
        wait_all(forward[g])
        span = pl.ds(g * size, size)
        base = me * per_rep + g * per_group
        a = jnp.concatenate([agg_in[q, span] for q in range(reps)], axis=1)
        pre = jnp.dot(a, weight[...], preferred_element_type=F32)
        mask = jnp.concatenate([row_mask(occ[base + j], slots) for j in range(per_group)], axis=0)
        sig = 0.5 * jnp.tanh(0.5 * pre) + 0.5
        o = (mask * (pre * sig)).astype(BF16)
        c = jnp.concatenate([cot[q, span] for q in range(reps)], axis=1).astype(F32)
        slope = (c * mask * sig * (1.0 + pre * (1.0 - sig))).astype(BF16)
        slope_all[span] = slope
        back = lax.dot_general(
            slope, weight[...], (((1,), (1,)), ((), ())), preferred_element_type=F32
        )
        s = scale[pl.ds(base, per_group)].reshape(size, part)
        for q in range(reps):
            cols = slice(q * part, (q + 1) * part)
            out_all[q, span] = o[:, cols]
            back_all[q, span] = (back[:, cols] * s).astype(BF16)
        backward += start_all(copies_of(g, back_all, up, send2, recv2))
    ends = []
    for d in range(reps):
        peer = lax.rem(me + d, reps)
        ends.append(pltpu.make_async_copy(out_all.at[peer], outs[d], stores.at[0, d]))
    start_all(ends)
    for q in range(reps):
        term = lax.dot_general(
            agg_in[q], slope_all[...], (((0,), (0,)), ((), ())), preferred_element_type=F32
        )
        wgrad[q] = term.astype(BF16)
    for d in range(reps):
        peer = lax.rem(me + d, reps)
        copy = pltpu.make_async_copy(wgrad.at[peer], wgrads[d], stores.at[1, d])
        copy.start()
        ends.append(copy)
    wait_all(ends)
    wait_all(backward)


def core(neigh, occupancy, scaled, incoming, scale, adjacency, cot, weight, collective_id):
    cells, _, slots, _ = adjacency.shape
    reps, rows, part = cot.shape
    groups = 4
    width = weight.shape[1]
    any_spec = pl.BlockSpec(memory_space=pl.ANY)
    results = pl.pallas_call(
        functools.partial(core_body, groups),
        in_specs=[pl.BlockSpec(memory_space=SMEM)] * 2 + [any_spec] * 6,
        out_specs=[any_spec] * (1 + 2 * reps),
        out_shape=[jax.ShapeDtypeStruct(cot.shape, BF16)]
        + [jax.ShapeDtypeStruct((rows, part), BF16)] * reps
        + [jax.ShapeDtypeStruct((part, width), BF16)] * reps,
        scratch_shapes=[
            VMEM((cells + incoming.shape[0], slots, part), BF16),
            VMEM(scale.shape, F32),
            VMEM(adjacency.shape, BF16),
            VMEM(cot.shape, BF16),
            VMEM(weight.shape, BF16),
            VMEM(cot.shape, BF16),
            VMEM(cot.shape, BF16),
            VMEM((rows, width), BF16),
            VMEM(cot.shape, BF16),
            VMEM(cot.shape, BF16),
            VMEM((reps, part, width), BF16),
            dma(5),
            dma(groups, reps),
            dma(groups, reps),
            dma(groups, reps),
            dma(groups, reps),
            dma(groups, reps),
            dma(2, reps),
        ],
        compiler_params=params(collective_id=collective_id, has_side_effects=True),
        name="core",
    )(neigh, occupancy, scaled, incoming, scale, adjacency, cot, weight)
    return results[0], results[1 : 1 + reps], results[1 + reps :]


def last_body(factor, cut, reps, terms, *refs):
    wgrads, returned, grad = refs[:reps], refs[reps], refs[reps + 1]
    rest = refs[reps + 2 :]
    greet(("rows",))
    peers = lax.axis_size("rows")
    me = lax.axis_index("rows")
    total = wgrads[0][...].astype(F32)
    for q in range(1, reps):
        total += wgrads[q][...].astype(F32)
    if not cut:
        grad[...] = total
        wait_all(start_all(exchange_copies("rows", terms, returned, rest[0], rest[1])))
        return
    held, parts = rest[2], rest[3]
    held[...] = total.astype(BF16).reshape(held.shape)
    sums = start_all(exchange_copies("rows", held, parts, rest[4], rest[5]))
    others = start_all(exchange_copies("rows", terms, returned, rest[0], rest[1]))
    wait_all(sums)
    total = parts[0].astype(F32)
    for p in range(1, peers):
        total += parts[p].astype(F32)
    grad[me] = total * factor
    copies = []
    for d in range(1, peers):
        copies.append(
            pltpu.make_async_remote_copy(
                src_ref=grad.at[me],
                dst_ref=grad.at[me],
                send_sem=rest[6].at[d],
                recv_sem=rest[7].at[d],
                device_id={"rows": lax.rem(me + d, peers)},
                device_id_type=MESH,
            )
        )
    wait_all(start_all(copies))
    wait_all(others)


def last_exchange(terms, wgrads, factor, collective_id):
    peers, reps = lax.axis_size("rows"), len(wgrads)
    part, width = wgrads[0].shape
    cut = part % (16 * peers) == 0
    scratch = [dma(peers), dma(peers)]
    grad_shape = (part, width)
    if cut:
        grad_shape = (peers, part // peers, width)
        scratch += [VMEM(grad_shape, BF16)] * 2 + [dma(peers)] * 4
    returned, grad = pl.pallas_call(
        functools.partial(last_body, factor, cut, reps),
        in_specs=[pl.BlockSpec(memory_space=pl.ANY)] + [pl.BlockSpec(memory_space=VMEM)] * reps,
        out_specs=[pl.BlockSpec(memory_space=pl.ANY), pl.BlockSpec(memory_space=VMEM)],
        out_shape=[
            jax.ShapeDtypeStruct(terms.shape, BF16),
            jax.ShapeDtypeStruct(grad_shape, F32),
        ],
        scratch_shapes=scratch,
        compiler_params=params(collective_id=collective_id, has_side_effects=True),
        name="last_exchange",
    )(terms, *wgrads)
    if not cut:
        grad = lax.psum(grad, "rows") * factor
    return returned, grad.reshape(part, width)


def combine_body(reps, send, occ, local, returned, scale, *refs):
    parts, out, output, total, sems = refs[:reps], *refs[reps:]
    me = lax.axis_index("rep")
    slots = local.shape[1]
    sending = returned.shape[1]
    moves = []
    for d in range(reps):
        place = lax.rem(me + (reps - d), reps)
        moves.append(pltpu.make_async_copy(parts[d], output.at[place], sems.at[d]))
    start_all(moves)
    total[...] = local[...]

    def add(t, carry):
        peer, place = t // sending, t % sending
        cell = send[0, peer, place]
        total[cell] = total[cell] + returned[peer, place].astype(F32)
        return carry

    lax.fori_loop(0, returned.shape[0] * sending, add, 0)

    def finish(i, carry):
        out[i] = (total[i] * (scale[i] * row_mask(occ[i], slots))).astype(BF16)
        return carry

    lax.fori_loop(0, local.shape[0], finish, 0)
    wait_all(moves)


def combine(send, occupancy, local, returned, scale, parts):
    reps = len(parts)
    vmem, hbm = pl.BlockSpec(memory_space=VMEM), pl.BlockSpec(memory_space=pl.ANY)
    return pl.pallas_call(
        functools.partial(combine_body, reps),
        in_specs=[pl.BlockSpec(memory_space=SMEM)] * 2 + [vmem] * 3 + [hbm] * reps,
        out_specs=[vmem, hbm],
        out_shape=[
            jax.ShapeDtypeStruct(local.shape, BF16),
            jax.ShapeDtypeStruct((reps,) + parts[0].shape, BF16),
        ],
        scratch_shapes=[VMEM(local.shape, F32), dma(reps)],
        compiler_params=params(),
        name="combine",
    )(send, occupancy, local, returned, scale, *parts)


def shifted(blocks):
    reps = len(blocks)
    moved = [blocks[0]]
    for d in range(1, reps):
        moved.append(lax.ppermute(blocks[d], "rep", [(i, (i + d) % reps) for i in range(reps)]))
    return moved


def on_device(features, adjacency, neighbours, occupancy, send_cells, weight, cotangent):
    cells, _, slots, _ = adjacency.shape
    part = features.shape[1]
    peers, reps = lax.axis_size("rows"), lax.axis_size("rep")
    sending = send_cells.shape[2]
    rows = cells * slots
    cell_shape = (cells, slots, part)
    cot = cotangent.reshape(reps, rows // reps, part)

    scale, scaled, incoming, cot_rows = prepare(
        features.reshape(cell_shape), adjacency, occupancy, send_cells, cot, 1
    )
    up, outs, wgrads = core(
        neighbours,
        occupancy,
        scaled,
        incoming.reshape(-1, slots, part),
        scale,
        adjacency,
        cot_rows,
        weight,
        2,
    )
    wgrads = shifted(wgrads)
    outs = shifted(outs)
    local, remote = spread(neighbours, up.reshape(cell_shape), adjacency, peers * sending)
    returned, weight_grad = last_exchange(
        remote.reshape(peers, sending, slots, part), wgrads, float(rows * peers) ** (-0.5), 3
    )
    feature_grad, output = combine(send_cells, occupancy, local, returned, scale, outs)
    return output.reshape(rows, part), weight_grad, feature_grad.reshape(rows, part)


def solution(mesh):
    placed = (
        P("rows", "rep"),
        P("rows", None, None, None),
        P("rows", None),
        P("rows"),
        P("rows", None, None),
        P(),
        P("rows", "rep"),
    )
    return jax.shard_map(
        on_device,
        mesh=mesh,
        in_specs=placed,
        out_specs=(P("rows", "rep"), P("rep", None), P("rows", "rep")),
        check_vma=False,
    )
```

```python
import functools

import jax
import jax.numpy as jnp
from jax import lax
from jax.experimental import pallas as pl
from jax.experimental.pallas import tpu as pltpu
from jax.sharding import PartitionSpec as P

MESH = pl.DeviceIdType.MESH
F32 = jnp.float32
BF16 = jnp.bfloat16
SMEM = pltpu.SMEM
VMEM = pltpu.VMEM


def params(**kw):
    return pltpu.CompilerParams(vmem_limit_bytes=56 * 1024 * 1024, **kw)


def whole_block(shape):
    return pl.BlockSpec(shape, lambda *_: (0,) * len(shape))


def row_mask(count, slots):
    rows = lax.broadcasted_iota(jnp.int32, (slots, 1), 0)
    return jnp.where(rows < count, 1.0, 0.0).astype(F32)


def spread_body(step_cells, neigh, up, adj, local, remote, table):
    step = pl.program_id(0)
    blocks, slots = adj.shape[1], adj.shape[2]

    @pl.when(step == 0)
    def _():
        table[...] = jnp.zeros_like(table)

    for j in range(step_cells):
        cell = step * step_cells + j
        wide = jnp.concatenate([adj[j, k] for k in range(blocks)], axis=1)
        terms = lax.dot_general(wide, up[j], (((0,), (0,)), ((), ())), preferred_element_type=F32)
        for k in range(blocks):
            slot = neigh[cell, k]
            table[slot] = table[slot] + terms[k * slots : (k + 1) * slots]

    @pl.when(step == pl.num_programs(0) - 1)
    def _():
        cells = local.shape[0]
        local[...] = table[pl.ds(0, cells)]
        remote[...] = table[pl.ds(cells, remote.shape[0])].astype(BF16)


def spread(neigh, up, adjacency, received):
    cells, blocks, slots, _ = adjacency.shape
    part = up.shape[2]
    n = 4
    return pl.pallas_call(
        functools.partial(spread_body, n),
        grid=(cells // n,),
        in_specs=[
            pl.BlockSpec(memory_space=SMEM),
            pl.BlockSpec((n, slots, part), lambda i: (i, 0, 0)),
            pl.BlockSpec((n, blocks, slots, slots), lambda i: (i, 0, 0, 0)),
        ],
        out_specs=[whole_block((cells, slots, part)), whole_block((received, slots, part))],
        out_shape=[
            jax.ShapeDtypeStruct((cells, slots, part), F32),
            jax.ShapeDtypeStruct((received, slots, part), BF16),
        ],
        scratch_shapes=[VMEM((cells + received, slots, part), F32)],
        compiler_params=params(),
        cost_estimate=pl.CostEstimate(
            flops=2 * adjacency.size * part,
            bytes_accessed=30_000_000,
            transcendentals=0,
        ),
        name="spread",
    )(neigh, up, adjacency)


def greet(axes):
    barrier = pltpu.get_barrier_semaphore()
    expected = 0
    for axis in axes:
        size = lax.axis_size(axis)
        me = lax.axis_index(axis)
        for d in range(1, size):
            pl.semaphore_signal(
                barrier, inc=1, device_id={axis: lax.rem(me + d, size)}, device_id_type=MESH
            )
        expected += size - 1
    pl.semaphore_wait(barrier, expected)


def exchange_copies(axis, src, dst, sends, recvs):
    size = lax.axis_size(axis)
    me = lax.axis_index(axis)
    copies = []
    for d in range(1, size):
        peer = lax.rem(me + d, size)
        copies.append(
            pltpu.make_async_remote_copy(
                src_ref=src.at[peer],
                dst_ref=dst.at[me],
                send_sem=sends.at[d],
                recv_sem=recvs.at[d],
                device_id={axis: peer},
                device_id_type=MESH,
            )
        )
    copies.append(pltpu.make_async_copy(src.at[me], dst.at[me], recvs.at[0]))
    return copies


def start_all(copies):
    for copy in copies:
        copy.start()
    return copies


def wait_all(copies):
    for copy in copies:
        copy.wait()


def dma(*shape):
    return pltpu.SemaphoreType.DMA(shape)


def prepare_body(
    step_cells, occ, send, feat, adj, cot, scale_out, scaled_out, incoming, cot_in, outgoing, *sems
):
    step = pl.program_id(0)
    slots = adj.shape[2]
    sending = outgoing.shape[1]

    @pl.when(step == 0)
    def _():
        greet(("rep", "rows"))
        start_all(exchange_copies("rep", cot, cot_in, sems[0], sems[1]))

    for j in range(step_cells):
        cell = step * step_cells + j
        total = jnp.zeros((slots, slots), F32)
        for k in range(adj.shape[1]):
            a = adj[j, k].astype(F32)
            total += a * a
        scale = lax.rsqrt(jnp.sqrt(jnp.sum(total, axis=1, keepdims=True) + 1e-6))
        scale_out[j] = jnp.broadcast_to(scale, scale_out.shape[1:])
        keep = scale * row_mask(occ[cell], slots)
        scaled_out[cell] = (feat[j].astype(F32) * keep).astype(BF16)

    @pl.when(step == pl.num_programs(0) - 1)
    def _():
        def put(t, carry):
            peer, place = t // sending, t % sending
            outgoing[peer, place] = scaled_out[send[0, peer, place]]
            return carry

        lax.fori_loop(0, outgoing.shape[0] * sending, put, 0)
        copies = start_all(exchange_copies("rows", outgoing, incoming, sems[2], sems[3]))
        wait_all(copies)
        wait_all(exchange_copies("rep", cot, cot_in, sems[0], sems[1]))


def prepare(features, adjacency, occupancy, send, cot, collective_id):
    cells, blocks, slots, _ = adjacency.shape
    part = features.shape[2]
    n = 4
    _, peers, sending = send.shape
    table = (peers, sending, slots, part)
    reps = cot.shape[0]
    return pl.pallas_call(
        functools.partial(prepare_body, n),
        grid=(cells // n,),
        in_specs=[
            pl.BlockSpec(memory_space=SMEM),
            pl.BlockSpec(memory_space=SMEM),
            pl.BlockSpec((n, slots, part), lambda i: (i, 0, 0)),
            pl.BlockSpec((n, blocks, slots, slots), lambda i: (i, 0, 0, 0)),
            pl.BlockSpec(memory_space=VMEM),
        ],
        out_specs=[
            pl.BlockSpec((n, slots, part), lambda i: (i, 0, 0)),
            whole_block((cells, slots, part)),
            pl.BlockSpec(memory_space=pl.ANY),
            pl.BlockSpec(memory_space=pl.ANY),
        ],
        out_shape=[
            jax.ShapeDtypeStruct((cells, slots, part), F32),
            jax.ShapeDtypeStruct((cells, slots, part), BF16),
            jax.ShapeDtypeStruct(table, BF16),
            jax.ShapeDtypeStruct(cot.shape, BF16),
        ],
        scratch_shapes=[VMEM(table, BF16), dma(reps), dma(reps), dma(peers), dma(peers)],
        compiler_params=params(collective_id=collective_id, has_side_effects=True),
        name="prepare",
    )(occupancy, send, features, adjacency, cot)


def core_body(groups, neigh, occ, scaled_h, incoming_h, scale_h, adj_h, cot_h, weight_h, *refs):
    reps, rows, part = cot_h.shape
    up, out_all, wgrad = refs[:3]
    table, scale, adj, cot, weight, agg, agg_in, slope_all, back_all = refs[3:12]
    loads, adj_loads, send1, recv1, send2, recv2 = refs[12:]
    me = lax.axis_index("rep")
    cells, blocks, slots, _ = adj.shape
    per_rep = cells // reps
    per_group = per_rep // groups
    size = per_group * slots
    order = list(range(1, reps)) + [0]

    early = [
        pltpu.make_async_copy(scaled_h, table.at[pl.ds(0, cells)], loads.at[0]),
        pltpu.make_async_copy(
            incoming_h, table.at[pl.ds(cells, incoming_h.shape[0])], loads.at[1]
        ),
        pltpu.make_async_copy(scale_h, scale, loads.at[2]),
    ]
    start_all(early)
    adj_copies = {}
    for g in range(groups):
        for d in order:
            cell = lax.rem(me + d, reps) * per_rep + g * per_group
            span = pl.ds(cell, per_group)
            copy = pltpu.make_async_copy(adj_h.at[span], adj.at[span], adj_loads.at[g, d])
            copy.start()
            adj_copies[g, d] = copy
    late = start_all(
        [
            pltpu.make_async_copy(cot_h, cot, loads.at[3]),
            pltpu.make_async_copy(weight_h, weight, loads.at[4]),
        ]
    )
    greet(("rep",))
    wait_all(early)

    def copies_of(g, src, dst, sends, recvs):
        span = pl.ds(g * size, size)
        found = []
        for d in order:
            peer = lax.rem(me + d, reps)
            if d == 0:
                found.append(
                    pltpu.make_async_copy(src.at[me, span], dst.at[me, span], recvs.at[g, 0])
                )
                continue
            found.append(
                pltpu.make_async_remote_copy(
                    src_ref=src.at[peer, span],
                    dst_ref=dst.at[me, span],
                    send_sem=sends.at[g, d],
                    recv_sem=recvs.at[g, d],
                    device_id={"rep": peer},
                    device_id_type=MESH,
                )
            )
        return found

    forward = []
    for g in range(groups):
        copies = copies_of(g, agg, agg_in, send1, recv1)
        for i, d in enumerate(order):
            peer = lax.rem(me + d, reps)
            adj_copies[g, d].wait()
            for j in range(per_group):
                cell = peer * per_rep + g * per_group + j
                near = jnp.concatenate([table[neigh[cell, k]] for k in range(blocks)], axis=0)
                wide = jnp.concatenate([adj[cell, k] for k in range(blocks)], axis=1)
                total = jnp.dot(wide, near, preferred_element_type=F32)
                agg[peer, pl.ds(g * size + j * slots, slots)] = (total * scale[cell]).astype(BF16)
            copies[i].start()
        forward.append(copies)
    wait_all(late)
    backward = []
    for g in range(groups):
        wait_all(forward[g])
        span = pl.ds(g * size, size)
        base = me * per_rep + g * per_group
        a = jnp.concatenate([agg_in[q, span] for q in range(reps)], axis=1)
        pre = jnp.dot(a, weight[...], preferred_element_type=F32)
        mask = jnp.concatenate([row_mask(occ[base + j], slots) for j in range(per_group)], axis=0)
        sig = 0.5 * jnp.tanh(0.5 * pre) + 0.5
        o = (mask * (pre * sig)).astype(BF16)
        c = jnp.concatenate([cot[q, span] for q in range(reps)], axis=1).astype(F32)
        slope = (c * mask * sig * (1.0 + pre * (1.0 - sig))).astype(BF16)
        slope_all[span] = slope
        back = lax.dot_general(
            slope, weight[...], (((1,), (1,)), ((), ())), preferred_element_type=F32
        )
        s = scale[pl.ds(base, per_group)].reshape(size, part)
        for q in range(reps):
            cols = slice(q * part, (q + 1) * part)
            out_all[q, span] = o[:, cols]
            back_all[q, span] = (back[:, cols] * s).astype(BF16)
        backward += start_all(copies_of(g, back_all, up, send2, recv2))
    for q in range(reps):
        term = lax.dot_general(
            agg_in[q], slope_all[...], (((0,), (0,)), ((), ())), preferred_element_type=F32
        )
        wgrad[q] = term.astype(BF16)
    wait_all(backward)


def core(neigh, occupancy, scaled, incoming, scale, adjacency, cot, weight, collective_id):
    cells, _, slots, _ = adjacency.shape
    reps, rows, part = cot.shape
    groups = 4
    width = weight.shape[1]
    any_spec = pl.BlockSpec(memory_space=pl.ANY)
    return pl.pallas_call(
        functools.partial(core_body, groups),
        in_specs=[pl.BlockSpec(memory_space=SMEM)] * 2 + [any_spec] * 6,
        out_specs=[any_spec] + [pl.BlockSpec(memory_space=VMEM)] * 2,
        out_shape=[
            jax.ShapeDtypeStruct(cot.shape, BF16),
            jax.ShapeDtypeStruct(cot.shape, BF16),
            jax.ShapeDtypeStruct((reps, part, width), BF16),
        ],
        scratch_shapes=[
            VMEM((cells + incoming.shape[0], slots, part), BF16),
            VMEM(scale.shape, F32),
            VMEM(adjacency.shape, BF16),
            VMEM(cot.shape, BF16),
            VMEM(weight.shape, BF16),
            VMEM(cot.shape, BF16),
            VMEM(cot.shape, BF16),
            VMEM((rows, width), BF16),
            VMEM(cot.shape, BF16),
            dma(5),
            dma(groups, reps),
            dma(groups, reps),
            dma(groups, reps),
            dma(groups, reps),
            dma(groups, reps),
        ],
        compiler_params=params(collective_id=collective_id, has_side_effects=True),
        name="core",
    )(neigh, occupancy, scaled, incoming, scale, adjacency, cot, weight)


def last_body(factor, cut, terms, out_rows, wgrad, returned, out, grad, ph1, *sems):
    greet(("rep", "rows"))
    peers = lax.axis_size("rows")
    me = lax.axis_index("rows")
    first = start_all(exchange_copies("rep", wgrad, ph1, sems[0], sems[1]))
    others = start_all(exchange_copies("rows", terms, returned, sems[2], sems[3]))
    wait_all(first)
    others += start_all(exchange_copies("rep", out_rows, out, sems[4], sems[5]))
    total = ph1[0].astype(F32)
    for q in range(1, ph1.shape[0]):
        total += ph1[q].astype(F32)
    if not cut:
        grad[...] = total
        wait_all(others)
        return
    held, parts = sems[6], sems[7]
    held[...] = total.astype(BF16).reshape(held.shape)
    wait_all(start_all(exchange_copies("rows", held, parts, sems[8], sems[9])))
    total = parts[0].astype(F32)
    for p in range(1, peers):
        total += parts[p].astype(F32)
    grad[me] = total * factor
    copies = []
    for d in range(1, peers):
        copies.append(
            pltpu.make_async_remote_copy(
                src_ref=grad.at[me],
                dst_ref=grad.at[me],
                send_sem=sems[10].at[d],
                recv_sem=sems[11].at[d],
                device_id={"rows": lax.rem(me + d, peers)},
                device_id_type=MESH,
            )
        )
    wait_all(start_all(copies))
    wait_all(others)


def last_exchange(terms, out_rows, wgrad, factor, collective_id):
    peers = lax.axis_size("rows")
    reps, part, width = wgrad.shape
    cut = part % (16 * peers) == 0
    scratch = [VMEM(wgrad.shape, BF16)] + [dma(reps)] * 2 + [dma(peers)] * 2 + [dma(reps)] * 2
    grad_shape = (part, width)
    if cut:
        grad_shape = (peers, part // peers, width)
        scratch += [VMEM(grad_shape, BF16)] * 2 + [dma(peers)] * 4
    vmem = pl.BlockSpec(memory_space=VMEM)
    returned, out, grad = pl.pallas_call(
        functools.partial(last_body, factor, cut),
        in_specs=[vmem] * 3,
        out_specs=[vmem, pl.BlockSpec(memory_space=pl.ANY), vmem],
        out_shape=[
            jax.ShapeDtypeStruct(terms.shape, BF16),
            jax.ShapeDtypeStruct(out_rows.shape, BF16),
            jax.ShapeDtypeStruct(grad_shape, F32),
        ],
        scratch_shapes=scratch,
        compiler_params=params(collective_id=collective_id, has_side_effects=True),
        name="last_exchange",
    )(terms, out_rows, wgrad)
    if not cut:
        grad = lax.psum(grad, "rows") * factor
    return returned, out, grad.reshape(part, width)


def combine_body(send, occ, local, returned, scale, out, total):
    slots = local.shape[1]
    sending = returned.shape[1]
    total[...] = local[...]

    def add(t, carry):
        peer, place = t // sending, t % sending
        cell = send[0, peer, place]
        total[cell] = total[cell] + returned[peer, place].astype(F32)
        return carry

    lax.fori_loop(0, returned.shape[0] * sending, add, 0)

    def finish(i, carry):
        out[i] = (total[i] * (scale[i] * row_mask(occ[i], slots))).astype(BF16)
        return carry

    lax.fori_loop(0, local.shape[0], finish, 0)


def combine(send, occupancy, local, returned, scale):
    vmem = pl.BlockSpec(memory_space=VMEM)
    return pl.pallas_call(
        combine_body,
        in_specs=[pl.BlockSpec(memory_space=SMEM)] * 2 + [vmem] * 3,
        out_specs=vmem,
        out_shape=jax.ShapeDtypeStruct(local.shape, BF16),
        scratch_shapes=[VMEM(local.shape, F32)],
        compiler_params=params(),
        name="combine",
    )(send, occupancy, local, returned, scale)


def on_device(features, adjacency, neighbours, occupancy, send_cells, weight, cotangent):
    cells, _, slots, _ = adjacency.shape
    part = features.shape[1]
    peers, reps = lax.axis_size("rows"), lax.axis_size("rep")
    sending = send_cells.shape[2]
    rows = cells * slots
    cell_shape = (cells, slots, part)
    cot = cotangent.reshape(reps, rows // reps, part)

    scale, scaled, incoming, cot_rows = prepare(
        features.reshape(cell_shape), adjacency, occupancy, send_cells, cot, 1
    )
    up, out_rows, wgrad = core(
        neighbours,
        occupancy,
        scaled,
        incoming.reshape(-1, slots, part),
        scale,
        adjacency,
        cot_rows,
        weight,
        2,
    )
    local, remote = spread(neighbours, up.reshape(cell_shape), adjacency, peers * sending)
    returned, output, weight_grad = last_exchange(
        remote.reshape(peers, sending, slots, part),
        out_rows,
        wgrad,
        float(rows * peers) ** (-0.5),
        3,
    )
    feature_grad = combine(send_cells, occupancy, local, returned, scale)
    return output.reshape(rows, part), weight_grad, feature_grad.reshape(rows, part)


def solution(mesh):
    placed = (
        P("rows", "rep"),
        P("rows", None, None, None),
        P("rows", None),
        P("rows"),
        P("rows", None, None),
        P(),
        P("rows", "rep"),
    )
    return jax.shard_map(
        on_device,
        mesh=mesh,
        in_specs=placed,
        out_specs=(P("rows", "rep"), P("rep", None), P("rows", "rep")),
        check_vma=False,
    )
```

```python
import functools

import jax
import jax.numpy as jnp
from jax import lax
from jax.experimental import pallas as pl
from jax.experimental.pallas import tpu as pltpu
from jax.sharding import PartitionSpec as P

MESH = pl.DeviceIdType.MESH
F32 = jnp.float32
BF16 = jnp.bfloat16
SMEM = pltpu.SMEM
VMEM = pltpu.VMEM


def params(**kw):
    return pltpu.CompilerParams(vmem_limit_bytes=56 * 1024 * 1024, **kw)


def whole_block(shape):
    return pl.BlockSpec(shape, lambda *_: (0,) * len(shape))


def row_mask(count, slots):
    rows = lax.broadcasted_iota(jnp.int32, (slots, 1), 0)
    return jnp.where(rows < count, 1.0, 0.0).astype(F32)


def spread_body(step_cells, neigh, up, adj, local, remote, table):
    step = pl.program_id(0)
    blocks, slots = adj.shape[1], adj.shape[2]

    @pl.when(step == 0)
    def _():
        table[...] = jnp.zeros_like(table)

    for j in range(step_cells):
        cell = step * step_cells + j
        wide = jnp.concatenate([adj[j, k] for k in range(blocks)], axis=1)
        terms = lax.dot_general(wide, up[j], (((0,), (0,)), ((), ())), preferred_element_type=F32)
        for k in range(blocks):
            slot = neigh[cell, k]
            table[slot] = table[slot] + terms[k * slots : (k + 1) * slots]

    @pl.when(step == pl.num_programs(0) - 1)
    def _():
        cells = local.shape[0]
        local[...] = table[pl.ds(0, cells)]
        remote[...] = table[pl.ds(cells, remote.shape[0])].astype(BF16)


def spread(neigh, up, adjacency, received):
    cells, blocks, slots, _ = adjacency.shape
    part = up.shape[2]
    n = 4
    return pl.pallas_call(
        functools.partial(spread_body, n),
        grid=(cells // n,),
        in_specs=[
            pl.BlockSpec(memory_space=SMEM),
            pl.BlockSpec((n, slots, part), lambda i: (i, 0, 0)),
            pl.BlockSpec((n, blocks, slots, slots), lambda i: (i, 0, 0, 0)),
        ],
        out_specs=[whole_block((cells, slots, part)), whole_block((received, slots, part))],
        out_shape=[
            jax.ShapeDtypeStruct((cells, slots, part), F32),
            jax.ShapeDtypeStruct((received, slots, part), BF16),
        ],
        scratch_shapes=[VMEM((cells + received, slots, part), F32)],
        compiler_params=params(),
        cost_estimate=pl.CostEstimate(
            flops=2 * adjacency.size * part,
            bytes_accessed=30_000_000,
            transcendentals=0,
        ),
        name="spread",
    )(neigh, up, adjacency)


def greet(axes):
    barrier = pltpu.get_barrier_semaphore()
    expected = 0
    for axis in axes:
        size = lax.axis_size(axis)
        me = lax.axis_index(axis)
        for d in range(1, size):
            pl.semaphore_signal(
                barrier, inc=1, device_id={axis: lax.rem(me + d, size)}, device_id_type=MESH
            )
        expected += size - 1
    pl.semaphore_wait(barrier, expected)


def exchange_copies(axis, src, dst, sends, recvs):
    size = lax.axis_size(axis)
    me = lax.axis_index(axis)
    copies = []
    for d in range(1, size):
        peer = lax.rem(me + d, size)
        copies.append(
            pltpu.make_async_remote_copy(
                src_ref=src.at[peer],
                dst_ref=dst.at[me],
                send_sem=sends.at[d],
                recv_sem=recvs.at[d],
                device_id={axis: peer},
                device_id_type=MESH,
            )
        )
    copies.append(pltpu.make_async_copy(src.at[me], dst.at[me], recvs.at[0]))
    return copies


def start_all(copies):
    for copy in copies:
        copy.start()
    return copies


def wait_all(copies):
    for copy in copies:
        copy.wait()


def dma(*shape):
    return pltpu.SemaphoreType.DMA(shape)


def prepare_body(
    step_cells, occ, send, feat, adj, cot, scale_out, scaled_out, incoming, cot_in, outgoing, *sems
):
    step = pl.program_id(0)
    slots = adj.shape[2]
    sending = outgoing.shape[1]

    @pl.when(step == 0)
    def _():
        greet(("rep", "rows"))
        start_all(exchange_copies("rep", cot, cot_in, sems[0], sems[1]))

    for j in range(step_cells):
        cell = step * step_cells + j
        total = jnp.zeros((slots, slots), F32)
        for k in range(adj.shape[1]):
            a = adj[j, k].astype(F32)
            total += a * a
        scale = lax.rsqrt(jnp.sqrt(jnp.sum(total, axis=1, keepdims=True) + 1e-6))
        scale_out[j] = jnp.broadcast_to(scale, scale_out.shape[1:])
        keep = scale * row_mask(occ[cell], slots)
        scaled_out[cell] = (feat[j].astype(F32) * keep).astype(BF16)

    @pl.when(step == pl.num_programs(0) - 1)
    def _():
        def put(t, carry):
            peer, place = t // sending, t % sending
            outgoing[peer, place] = scaled_out[send[0, peer, place]]
            return carry

        lax.fori_loop(0, outgoing.shape[0] * sending, put, 0)
        copies = start_all(exchange_copies("rows", outgoing, incoming, sems[2], sems[3]))
        wait_all(copies)
        wait_all(exchange_copies("rep", cot, cot_in, sems[0], sems[1]))


def prepare(features, adjacency, occupancy, send, cot, collective_id):
    cells, blocks, slots, _ = adjacency.shape
    part = features.shape[2]
    n = 4
    _, peers, sending = send.shape
    table = (peers, sending, slots, part)
    reps = cot.shape[0]
    return pl.pallas_call(
        functools.partial(prepare_body, n),
        grid=(cells // n,),
        in_specs=[
            pl.BlockSpec(memory_space=SMEM),
            pl.BlockSpec(memory_space=SMEM),
            pl.BlockSpec((n, slots, part), lambda i: (i, 0, 0)),
            pl.BlockSpec((n, blocks, slots, slots), lambda i: (i, 0, 0, 0)),
            pl.BlockSpec(memory_space=VMEM),
        ],
        out_specs=[
            pl.BlockSpec((n, slots, part), lambda i: (i, 0, 0)),
            whole_block((cells, slots, part)),
            pl.BlockSpec(memory_space=pl.ANY),
            pl.BlockSpec(memory_space=pl.ANY),
        ],
        out_shape=[
            jax.ShapeDtypeStruct((cells, slots, part), F32),
            jax.ShapeDtypeStruct((cells, slots, part), BF16),
            jax.ShapeDtypeStruct(table, BF16),
            jax.ShapeDtypeStruct(cot.shape, BF16),
        ],
        scratch_shapes=[VMEM(table, BF16), dma(reps), dma(reps), dma(peers), dma(peers)],
        compiler_params=params(collective_id=collective_id, has_side_effects=True),
        name="prepare",
    )(occupancy, send, features, adjacency, cot)


def core_body(groups, neigh, occ, scaled_h, incoming_h, scale_h, adj_h, cot_h, weight_h, *refs):
    reps, rows, part = cot_h.shape
    up, out_all, grads = refs[:3]
    table, scale, adj, cot, weight, agg, agg_in, slope_all, back_all, wgrad = refs[3:13]
    loads, adj_loads, send1, recv1, send2, recv2, send3, recv3 = refs[13:]
    me = lax.axis_index("rep")
    cells, blocks, slots, _ = adj.shape
    per_rep = cells // reps
    per_group = per_rep // groups
    size = per_group * slots
    order = list(range(1, reps)) + [0]

    early = [
        pltpu.make_async_copy(scaled_h, table.at[pl.ds(0, cells)], loads.at[0]),
        pltpu.make_async_copy(
            incoming_h, table.at[pl.ds(cells, incoming_h.shape[0])], loads.at[1]
        ),
        pltpu.make_async_copy(scale_h, scale, loads.at[2]),
    ]
    start_all(early)
    adj_copies = {}
    for g in range(groups):
        for d in order:
            cell = lax.rem(me + d, reps) * per_rep + g * per_group
            span = pl.ds(cell, per_group)
            copy = pltpu.make_async_copy(adj_h.at[span], adj.at[span], adj_loads.at[g, d])
            copy.start()
            adj_copies[g, d] = copy
    late = start_all(
        [
            pltpu.make_async_copy(cot_h, cot, loads.at[3]),
            pltpu.make_async_copy(weight_h, weight, loads.at[4]),
        ]
    )
    greet(("rep",))
    wait_all(early)

    def copies_of(g, src, dst, sends, recvs):
        span = pl.ds(g * size, size)
        found = []
        for d in order:
            peer = lax.rem(me + d, reps)
            if d == 0:
                found.append(
                    pltpu.make_async_copy(src.at[me, span], dst.at[me, span], recvs.at[g, 0])
                )
                continue
            found.append(
                pltpu.make_async_remote_copy(
                    src_ref=src.at[peer, span],
                    dst_ref=dst.at[me, span],
                    send_sem=sends.at[g, d],
                    recv_sem=recvs.at[g, d],
                    device_id={"rep": peer},
                    device_id_type=MESH,
                )
            )
        return found

    forward = []
    for g in range(groups):
        copies = copies_of(g, agg, agg_in, send1, recv1)
        for i, d in enumerate(order):
            peer = lax.rem(me + d, reps)
            adj_copies[g, d].wait()
            for j in range(per_group):
                cell = peer * per_rep + g * per_group + j
                near = jnp.concatenate([table[neigh[cell, k]] for k in range(blocks)], axis=0)
                wide = jnp.concatenate([adj[cell, k] for k in range(blocks)], axis=1)
                total = jnp.dot(wide, near, preferred_element_type=F32)
                agg[peer, pl.ds(g * size + j * slots, slots)] = (total * scale[cell]).astype(BF16)
            copies[i].start()
        forward.append(copies)
    wait_all(late)
    backward = []
    for g in range(groups):
        wait_all(forward[g])
        span = pl.ds(g * size, size)
        base = me * per_rep + g * per_group
        a = jnp.concatenate([agg_in[q, span] for q in range(reps)], axis=1)
        pre = jnp.dot(a, weight[...], preferred_element_type=F32)
        mask = jnp.concatenate([row_mask(occ[base + j], slots) for j in range(per_group)], axis=0)
        sig = 0.5 * jnp.tanh(0.5 * pre) + 0.5
        o = (mask * (pre * sig)).astype(BF16)
        c = jnp.concatenate([cot[q, span] for q in range(reps)], axis=1).astype(F32)
        slope = (c * mask * sig * (1.0 + pre * (1.0 - sig))).astype(BF16)
        slope_all[span] = slope
        back = lax.dot_general(
            slope, weight[...], (((1,), (1,)), ((), ())), preferred_element_type=F32
        )
        s = scale[pl.ds(base, per_group)].reshape(size, part)
        for q in range(reps):
            cols = slice(q * part, (q + 1) * part)
            out_all[q, span] = o[:, cols]
            back_all[q, span] = (back[:, cols] * s).astype(BF16)
        backward += start_all(copies_of(g, back_all, up, send2, recv2))
    for q in range(reps):
        term = lax.dot_general(
            agg_in[q], slope_all[...], (((0,), (0,)), ((), ())), preferred_element_type=F32
        )
        wgrad[q] = term.astype(BF16)
    backward += start_all(exchange_copies("rep", wgrad, grads, send3, recv3))
    wait_all(backward)


def core(neigh, occupancy, scaled, incoming, scale, adjacency, cot, weight, collective_id):
    cells, _, slots, _ = adjacency.shape
    reps, rows, part = cot.shape
    groups = 4
    width = weight.shape[1]
    any_spec = pl.BlockSpec(memory_space=pl.ANY)
    return pl.pallas_call(
        functools.partial(core_body, groups),
        in_specs=[pl.BlockSpec(memory_space=SMEM)] * 2 + [any_spec] * 6,
        out_specs=[any_spec] + [pl.BlockSpec(memory_space=VMEM)] * 2,
        out_shape=[
            jax.ShapeDtypeStruct(cot.shape, BF16),
            jax.ShapeDtypeStruct(cot.shape, BF16),
            jax.ShapeDtypeStruct((reps, part, width), BF16),
        ],
        scratch_shapes=[
            VMEM((cells + incoming.shape[0], slots, part), BF16),
            VMEM(scale.shape, F32),
            VMEM(adjacency.shape, BF16),
            VMEM(cot.shape, BF16),
            VMEM(weight.shape, BF16),
            VMEM(cot.shape, BF16),
            VMEM(cot.shape, BF16),
            VMEM((rows, width), BF16),
            VMEM(cot.shape, BF16),
            VMEM((reps, part, width), BF16),
            dma(5),
            dma(groups, reps),
            dma(groups, reps),
            dma(groups, reps),
            dma(groups, reps),
            dma(groups, reps),
            dma(reps),
            dma(reps),
        ],
        compiler_params=params(collective_id=collective_id, has_side_effects=True),
        name="core",
    )(neigh, occupancy, scaled, incoming, scale, adjacency, cot, weight)


def last_body(factor, cut, terms, out_rows, grads, returned, out, grad, *sems):
    greet(("rep", "rows"))
    peers = lax.axis_size("rows")
    me = lax.axis_index("rows")
    total = grads[0].astype(F32)
    for q in range(1, grads.shape[0]):
        total += grads[q].astype(F32)
    sums = []
    if cut:
        held, parts = sems[4], sems[5]
        held[...] = total.astype(BF16).reshape(held.shape)
        sums = start_all(exchange_copies("rows", held, parts, sems[6], sems[7]))
    mine = exchange_copies("rep", out_rows, out, sems[2], sems[3])
    others = []
    every = peers // len(mine)
    for i, copy in enumerate(exchange_copies("rows", terms, returned, sems[0], sems[1])):
        others.append(copy)
        if i % every == 0 and mine:
            others.append(mine.pop(0))
    others = start_all(others + mine)
    if not cut:
        grad[...] = total
        wait_all(others)
        return
    wait_all(sums)
    total = parts[0].astype(F32)
    for p in range(1, peers):
        total += parts[p].astype(F32)
    grad[me] = total * factor
    copies = []
    for d in range(1, peers):
        copies.append(
            pltpu.make_async_remote_copy(
                src_ref=grad.at[me],
                dst_ref=grad.at[me],
                send_sem=sems[8].at[d],
                recv_sem=sems[9].at[d],
                device_id={"rows": lax.rem(me + d, peers)},
                device_id_type=MESH,
            )
        )
    wait_all(start_all(copies))
    wait_all(others)


def last_exchange(terms, out_rows, wgrad, factor, collective_id):
    peers = lax.axis_size("rows")
    reps, part, width = wgrad.shape
    cut = part % (16 * peers) == 0
    scratch = [dma(peers)] * 2 + [dma(reps)] * 2
    grad_shape = (part, width)
    if cut:
        grad_shape = (peers, part // peers, width)
        scratch += [VMEM(grad_shape, BF16)] * 2 + [dma(peers)] * 4
    vmem = pl.BlockSpec(memory_space=VMEM)
    returned, out, grad = pl.pallas_call(
        functools.partial(last_body, factor, cut),
        in_specs=[vmem] * 3,
        out_specs=[vmem, pl.BlockSpec(memory_space=pl.ANY), vmem],
        out_shape=[
            jax.ShapeDtypeStruct(terms.shape, BF16),
            jax.ShapeDtypeStruct(out_rows.shape, BF16),
            jax.ShapeDtypeStruct(grad_shape, F32),
        ],
        scratch_shapes=scratch,
        compiler_params=params(collective_id=collective_id, has_side_effects=True),
        name="last_exchange",
    )(terms, out_rows, wgrad)
    if not cut:
        grad = lax.psum(grad, "rows") * factor
    return returned, out, grad.reshape(part, width)


def combine_body(send, occ, local, returned, scale, out, total):
    slots = local.shape[1]
    sending = returned.shape[1]
    total[...] = local[...]

    def add(t, carry):
        peer, place = t // sending, t % sending
        cell = send[0, peer, place]
        total[cell] = total[cell] + returned[peer, place].astype(F32)
        return carry

    lax.fori_loop(0, returned.shape[0] * sending, add, 0)

    def finish(i, carry):
        out[i] = (total[i] * (scale[i] * row_mask(occ[i], slots))).astype(BF16)
        return carry

    lax.fori_loop(0, local.shape[0], finish, 0)


def combine(send, occupancy, local, returned, scale):
    vmem = pl.BlockSpec(memory_space=VMEM)
    return pl.pallas_call(
        combine_body,
        in_specs=[pl.BlockSpec(memory_space=SMEM)] * 2 + [vmem] * 3,
        out_specs=vmem,
        out_shape=jax.ShapeDtypeStruct(local.shape, BF16),
        scratch_shapes=[VMEM(local.shape, F32)],
        compiler_params=params(),
        name="combine",
    )(send, occupancy, local, returned, scale)


def on_device(features, adjacency, neighbours, occupancy, send_cells, weight, cotangent):
    cells, _, slots, _ = adjacency.shape
    part = features.shape[1]
    peers, reps = lax.axis_size("rows"), lax.axis_size("rep")
    sending = send_cells.shape[2]
    rows = cells * slots
    cell_shape = (cells, slots, part)
    cot = cotangent.reshape(reps, rows // reps, part)

    scale, scaled, incoming, cot_rows = prepare(
        features.reshape(cell_shape), adjacency, occupancy, send_cells, cot, 1
    )
    up, out_rows, wgrad = core(
        neighbours,
        occupancy,
        scaled,
        incoming.reshape(-1, slots, part),
        scale,
        adjacency,
        cot_rows,
        weight,
        2,
    )
    local, remote = spread(neighbours, up.reshape(cell_shape), adjacency, peers * sending)
    returned, output, weight_grad = last_exchange(
        remote.reshape(peers, sending, slots, part),
        out_rows,
        wgrad,
        float(rows * peers) ** (-0.5),
        3,
    )
    feature_grad = combine(send_cells, occupancy, local, returned, scale)
    return output.reshape(rows, part), weight_grad, feature_grad.reshape(rows, part)


def solution(mesh):
    placed = (
        P("rows", "rep"),
        P("rows", None, None, None),
        P("rows", None),
        P("rows"),
        P("rows", None, None),
        P(),
        P("rows", "rep"),
    )
    return jax.shard_map(
        on_device,
        mesh=mesh,
        in_specs=placed,
        out_specs=(P("rows", "rep"), P("rep", None), P("rows", "rep")),
        check_vma=False,
    )
```
